1024 devices in a mesh: gx: 4 (over x), gy: 8 (over y, core), gz: 32 (over z).
Axes of the slice: x: 4, y: 4, z: 32, core: 2. Of those that a mesh axis runs over, the one named last changes fastest.
Arguments:
- thermal_level: float32 [256, 512, 512], P('gz', 'gy', 'gx'), may hold values from 0.3 to 2
- blend_fraction: float32 [256, 512, 512], P('gz', 'gy', 'gx'), may hold values from 0 to 1
- nonempty_blocks: int32 [256, 512, 4], P('gz', 'gy', 'gx'), may hold values 0 or 1
- appearance_weights: float32 [4, 7], replicated, may hold values from -4 to 4
- illumination_vector: float32 [3], replicated, may hold values from -4 to 4
Outputs:
- frame: float32 [4, 512, 512], P(None, ('gy', 'gz'), 'gx')
The draws below stay inside these ranges and needn't reach their ends.
All inputs are finite; a program needn't handle non-finite values. No bound on the sum of `nonempty_blocks` on one device may be relied on, other than what follows from the above.
Results may differ from the reference program's by a relative error of at most 0.0003.
Values sent between devices are 32-bit elements; how exact they have to be, the bound alone decides.
No kernel may reach another device: no remote copies, remote signals or barrier semaphores. Data moves between devices by JAX's collectives and lax.ppermute only.
A program may use at most 32 MiB of HBM per device.

```python
import jax
import jax.numpy as jnp
from jax import lax

WIDTH_SAMPLES = 512
HEIGHT_SAMPLES = 512
SAMPLES_SIGHTWARD = 256


def with_ends(entries, own_key, smallest, high):
    dims = entries.shape
    place = [jax.random.randint(jax.random.fold_in(own_key, axis), (), 0, dims[axis]) for axis in range(len(dims))]
    entries = entries.at[tuple(place)].set(smallest)
    longest = dims.index(max(dims))
    place[longest] = (place[longest] + 1) % dims[longest]
    return entries.at[tuple(place)].set(high)


def steps_of(rng, shape, split, low, high):
    level = 1.0
    for axis_at, shards_of in split:
        steps = jax.random.uniform(jax.random.fold_in(jax.random.fold_in(rng, 6), axis_at), (shards_of,), jnp.float32, low / len(split), high / len(split))
        level = level * jnp.repeat(jnp.exp(steps), shape[axis_at] // shards_of).reshape((-1,) + (1,) * (len(shape) - 1 - axis_at))
    return level


def noise(stream_key, dims, spread, most, kind=jnp.bfloat16):
    values = spread * jax.random.normal(stream_key, dims, jnp.float32)
    return jnp.clip(values, min=-most, max=most).astype(kind)


def setup_inputs(seed: int = 0) -> dict:
    splits = jax.random.split(jax.random.key(seed), 6)
    return {
        "thermal_level": jnp.clip(0.3 + 1.7 * jax.random.uniform(splits[0], (SAMPLES_SIGHTWARD, HEIGHT_SAMPLES, WIDTH_SAMPLES), jnp.float32) ** steps_of(splits[0], (SAMPLES_SIGHTWARD, HEIGHT_SAMPLES, WIDTH_SAMPLES), ((0, 32), (1, 8), (2, 4)), -0.2, 0.2), 0.3, 2.0),
        "blend_fraction": jnp.clip(1.0 * jax.random.uniform(splits[1], (SAMPLES_SIGHTWARD, HEIGHT_SAMPLES, WIDTH_SAMPLES), jnp.float32) ** steps_of(splits[1], (SAMPLES_SIGHTWARD, HEIGHT_SAMPLES, WIDTH_SAMPLES), ((0, 32), (1, 8), (2, 4)), -0.2, 0.2), 0.0, 1.0),
        "nonempty_blocks": with_ends((jax.random.randint(splits[2], (SAMPLES_SIGHTWARD, HEIGHT_SAMPLES, WIDTH_SAMPLES // 128), 0, 3) < 2).astype(jnp.int32), jax.random.fold_in(splits[2], 1), 0, 1),
        "appearance_weights": noise(splits[3], (4, 7), 1.0, 4.0, jnp.float32),
        "illumination_vector": noise(splits[4], (3,), 1.0, 4.0, jnp.float32),
    }


def midpoint_difference(slab_field):
    centre = slab_field[1:-1, 1:-1, 1:-1]
    grad_z = (slab_field[2:, 1:-1, 1:-1] - slab_field[:-2, 1:-1, 1:-1]) * 0.5
    grad_y = (slab_field[1:-1, 2:, 1:-1] - slab_field[1:-1, :-2, 1:-1]) * 0.5
    grad_x = (slab_field[1:-1, 1:-1, 2:] - slab_field[1:-1, 1:-1, :-2]) * 0.5
    return (centre, grad_z, grad_y, grad_x)

def illuminate_samples(sheet_heat, sheet_blend, filled_flags, appearance_weights, illumination_vector, march_spacing):
    heat_centred, heat_slope_forward, heat_slope_vertical, heat_slope_horizontal = midpoint_difference(sheet_heat)
    mix_c, mz_grad, my_grad, mx_grad = midpoint_difference(sheet_blend)
    temp_sq = heat_slope_forward * heat_slope_forward + heat_slope_vertical * heat_slope_vertical + heat_slope_horizontal * heat_slope_horizontal
    mix_sq = mz_grad * mz_grad + my_grad * my_grad + mx_grad * mx_grad
    lambert = (heat_slope_horizontal * illumination_vector[0] + heat_slope_vertical * illumination_vector[1] + heat_slope_forward * illumination_vector[2]) / jnp.sqrt(temp_sq + 1.0)
    features = [heat_centred, mix_c, temp_sq / (1.0 + temp_sq), mix_sq / (1.0 + mix_sq), lambert, heat_centred * mix_c]
    linear = []
    for row_id in range(4):
        total = appearance_weights[row_id, 6] + jnp.zeros_like(heat_centred)
        for feat_id in range(6):
            total = total + appearance_weights[row_id, feat_id] * features[feat_id]
        linear.append(total)
    emitted_hues = jnp.stack([jax.nn.sigmoid(linear[0]), jax.nn.sigmoid(linear[1]), jax.nn.sigmoid(linear[2])])
    extinction = jax.nn.softplus(linear[3]) * filled_flags
    attenuated_share = 1.0 - jnp.exp(-march_spacing * extinction)
    return (attenuated_share, emitted_hues)

def brick_image(attenuated_share, emitted_hues):
    kept = 1.0 - attenuated_share
    transmit = jnp.concatenate([jnp.ones_like(kept[:1]), jnp.cumprod(kept, axis=0)[:-1]], axis=0)
    weights = attenuated_share * transmit
    colour_sum = lax.optimization_barrier(jnp.sum(weights[None] * emitted_hues, axis=1))
    opacity = lax.optimization_barrier(jnp.sum(weights, axis=0))
    return jnp.concatenate([colour_sum, opacity[None]], axis=0)

def reference(thermal_level, blend_fraction, nonempty_blocks, appearance_weights, illumination_vector):
    march_spacing = 2.0 / SAMPLES_SIGHTWARD
    block_rows = 32
    block_count = HEIGHT_SAMPLES // block_rows

    def one_block(block_id):
        row_start = block_id * block_rows
        vertical_positions = jnp.clip(jnp.arange(-1, block_rows + 1, dtype=jnp.int32) + row_start, 0, HEIGHT_SAMPLES - 1).astype(jnp.int32)
        sheet_heat = jnp.pad(jnp.take(thermal_level, vertical_positions, axis=1), ((1, 1), (0, 0), (1, 1)), mode='edge')
        sheet_blend = jnp.pad(jnp.take(blend_fraction, vertical_positions, axis=1), ((1, 1), (0, 0), (1, 1)), mode='edge')
        occ_block = lax.dynamic_slice_in_dim(nonempty_blocks, row_start, block_rows, axis=1)
        filled_flags = jnp.repeat(occ_block, 128, axis=2).astype(jnp.float32)
        attenuated_share, emitted_hues = illuminate_samples(sheet_heat, sheet_blend, filled_flags, appearance_weights, illumination_vector, march_spacing)
        return brick_image(attenuated_share, emitted_hues)
    blocks = lax.map(one_block, jnp.arange(block_count, dtype=jnp.int32))
    return jnp.transpose(blocks, (1, 0, 2, 3)).reshape(4, HEIGHT_SAMPLES, WIDTH_SAMPLES)
```

```python
import jax
import jax.numpy as jnp
from jax import lax
from jax.experimental import pallas as pl
from jax.experimental.pallas import tpu as pltpu
from jax.sharding import PartitionSpec as P

EXACT = lax.Precision.HIGHEST
F32 = jnp.float32


def face_kernel(heat, blend, x_lo, x_hi, y_lo, y_hi, z_lo, z_hi):
    deep, tall, wide = heat.shape
    row = lax.broadcasted_iota(jnp.int32, (8, wide), 0)
    lane = lax.broadcasted_iota(jnp.int32, (8, wide), 1)
    pick = (((row == 0) & (lane == 0)) | ((row == 1) & (lane == wide - 1))).astype(F32)
    for index, field in enumerate((heat, blend)):
        flat = field[...].reshape(deep * tall, wide)
        ends = lax.dot_general(
            pick, flat, (((1,), (1,)), ((), ())), precision=EXACT, preferred_element_type=F32
        )
        x_lo[index : index + 1, :] = ends[0:1]
        x_hi[index : index + 1, :] = ends[1:2]
        for z in range(deep):
            y_lo[index, z : z + 1, :] = field[z, 0:1, :]
            y_hi[index, z : z + 1, :] = field[z, tall - 1 : tall, :]
        z_lo[index] = field[0]
        z_hi[index] = field[deep - 1]


def faces(heat, blend):
    deep, tall, wide = heat.shape
    shapes = [(2, deep * tall)] * 2 + [(2, deep, wide)] * 2 + [(2, tall, wide)] * 2
    return pl.pallas_call(
        face_kernel, out_shape=[jax.ShapeDtypeStruct(s, F32) for s in shapes], name="faces"
    )(heat, blend)


def brick_kernel(
    spacing, order, place, weights, light, heat, blend, filled, x_lo, x_hi, y_lo, y_hi, z_lo, z_hi,
    x_own_lo, x_own_hi, image, x_step,
):
    deep, tall, wide = heat.shape
    at = [place[i] == 1 for i in range(6)]
    row8 = lax.broadcasted_iota(jnp.int32, (8, wide), 0)
    lane8 = lax.broadcasted_iota(jnp.int32, (8, wide), 1)
    spread = jnp.where((row8 < 2) & (lane8 == 0), -1.0, 0.0) + jnp.where(
        (row8 >= 2) & (row8 < 4) & (lane8 == wide - 1), 1.0, 0.0
    )
    below = jnp.where(at[0], x_own_lo[...], x_lo[...])
    above = jnp.where(at[1], x_own_hi[...], x_hi[...])
    for index in range(2):
        keep = (row8 % 2 == index).astype(F32)
        sides = jnp.concatenate([below, above, jnp.zeros((4, deep * tall), F32)], axis=0)
        x_step[index] = lax.dot_general(
            sides, spread * keep, (((0,), (0,)), ((), ())), precision=EXACT,
            preferred_element_type=F32,
        ).reshape(deep, tall, wide)
    w = [[weights[r, k] for k in range(7)] for r in range(4)]
    sun = [light[i] for i in range(3)]
    fields = (heat, blend)
    not_first = lane8 > 0
    not_last = lane8 < wide - 1
    for block in range(tall // 8):
        top = 8 * block
        rows = slice(top, top + 8)
        through = jnp.ones((8, wide), F32)
        sums = [jnp.zeros((8, wide), F32) for _ in range(4)]

        def cells(index, z):
            if z < 0:
                return jnp.where(at[4], fields[index][0, rows, :], z_lo[index, rows, :])
            if z == deep:
                return jnp.where(at[5], fields[index][deep - 1, rows, :], z_hi[index, rows, :])
            return fields[index][z, rows, :]

        for z in range(deep):
            slopes = []
            for index in range(2):
                field = fields[index]
                here = field[z, rows, :]
                dz = cells(index, z + 1) - cells(index, z - 1)
                if block == 0:
                    edge = jnp.where(at[2], field[z, 0:1, :], y_lo[index, z : z + 1, :])
                    up = jnp.concatenate([edge, field[z, 0:7, :]], axis=0)
                else:
                    up = field[z, top - 1 : top + 7, :]
                if top + 8 == tall:
                    edge = jnp.where(at[3], field[z, tall - 1 : tall, :], y_hi[index, z : z + 1, :])
                    down = jnp.concatenate([field[z, top + 1 : tall, :], edge], axis=0)
                else:
                    down = field[z, top + 1 : top + 9, :]
                dy = down - up
                right = jnp.where(not_last, pltpu.roll(here, wide - 1, 1), 0.0)
                left = jnp.where(not_first, pltpu.roll(here, 1, 1), 0.0)
                dx = right - left + x_step[index, z, rows, :]
                slopes.append((here, dz * 0.5, dy * 0.5, dx * 0.5))
            t, tz, ty, tx = slopes[0]
            m, mz, my, mx = slopes[1]
            t_sq = tz * tz + ty * ty + tx * tx
            m_sq = mz * mz + my * my + mx * mx
            inverse = lax.rsqrt(t_sq + 1.0)
            features = [
                t,
                m,
                t_sq * (inverse * inverse),
                m_sq / (1.0 + m_sq),
                (tx * sun[0] + ty * sun[1] + tz * sun[2]) * inverse,
                t * m,
            ]
            linear = []
            for r in range(4):
                total = w[r][6] + w[r][0] * features[0]
                for k in range(1, 6):
                    total = total + w[r][k] * features[k]
                linear.append(total)
            hues = [0.5 * jnp.tanh(0.5 * linear[r]) + 0.5 for r in range(3)]
            soft = jnp.maximum(linear[3], 0.0) + jnp.log1p(jnp.exp(-jnp.abs(linear[3])))
            occupied = filled[z, rows, :].astype(F32)
            absorbed = 1.0 - jnp.exp(soft * (occupied * -spacing))
            weight = absorbed * through
            through = through * (1.0 - absorbed)
            for r in range(3):
                sums[r] = sums[r] + weight * hues[r]
            sums[3] = sums[3] + weight
        for j in range(4):
            for r in range(4):
                image[order[4 * block + j], 2 * r : 2 * r + 2, :] = sums[r][2 * j : 2 * j + 2]


def over_kernel(order, parts, frame):
    wide = parts.shape[2]
    row = lax.broadcasted_iota(jnp.int32, (8, wide), 0)
    through = jnp.ones((8, wide), F32)
    total = jnp.zeros((8, wide), F32)
    for z in range(parts.shape[0]):
        part = parts[order[z]]
        veil = jnp.where(row >= 6, part, 0.0)
        veil = veil + pltpu.roll(veil, 4, 0)
        veil = veil + pltpu.roll(veil, 2, 0)
        total = total + through * part
        through = through * (1.0 - veil)
    for r in range(4):
        frame[r] = total[2 * r : 2 * r + 2]


def on_device(heat, blend, filled, weights, light):
    deep, tall, wide = heat.shape
    depth_count = lax.axis_size("gz")
    spacing = 2.0 / (deep * depth_count)
    own = faces(heat, blend)
    halos, place = [], []
    for axis, lo, hi in (("gx", own[0], own[1]), ("gy", own[2], own[3]), ("gz", own[4], own[5])):
        count = lax.axis_size(axis)
        halos.append(lax.ppermute(hi, axis, [(i, i + 1) for i in range(count - 1)]))
        halos.append(lax.ppermute(lo, axis, [(i + 1, i) for i in range(count - 1)]))
        place += [lax.axis_index(axis) == 0, lax.axis_index(axis) == count - 1]
    place = jnp.stack(place).astype(jnp.int32)
    first = depth_count // 2
    group = [(first + i) % depth_count for i in range(depth_count)]
    order = [group.index(z) for z in range(depth_count)]
    smem = pl.BlockSpec(memory_space=pltpu.SMEM)
    vmem = pl.BlockSpec(memory_space=pltpu.VMEM)

    def brick(*refs):
        brick_kernel(spacing, order, *refs)

    def over(*refs):
        over_kernel(order, *refs)

    image = pl.pallas_call(
        brick,
        out_shape=jax.ShapeDtypeStruct((depth_count, 8, wide), F32),
        in_specs=[smem] * 3 + [vmem] * 11,
        scratch_shapes=[pltpu.VMEM((2, deep, tall, wide), F32)],
        name="brick",
    )(place, weights, light, heat, blend, filled, *halos, own[0], own[1])
    parts = lax.all_to_all(image, "gz", 0, 0, tiled=True, axis_index_groups=[group])
    return pl.pallas_call(
        over, out_shape=jax.ShapeDtypeStruct((4, tall // depth_count, wide), F32), name="over"
    )(parts)


def solution(mesh):
    placed = (P("gz", "gy", "gx"), P("gz", "gy", "gx"), P("gz", "gy", "gx"), P(), P())
    return jax.shard_map(
        on_device,
        mesh=mesh,
        in_specs=placed,
        out_specs=P(None, ("gy", "gz"), "gx"),
        check_vma=False,
    )
```

```python
import jax
import jax.numpy as jnp
from jax import lax
from jax.experimental import pallas as pl
from jax.experimental.pallas import tpu as pltpu
from jax.sharding import PartitionSpec as P

F32 = jnp.float32
SMALL = pltpu.CompilerParams(vmem_limit_bytes=8 * 2**20)


def face_kernel(heat, blend, x_lo, x_hi, y_lo, y_hi, z_lo, z_hi):
    deep, tall, wide = heat.shape
    for index, field in enumerate((heat, blend)):
        z_lo[index] = field[0]
        z_hi[index] = field[deep - 1]
        y_lo[index] = jnp.concatenate([field[z, 0:1, :] for z in range(deep)], axis=0)
        y_hi[index] = jnp.concatenate([field[z, tall - 1 : tall, :] for z in range(deep)], axis=0)
    lane = lax.broadcasted_iota(jnp.int32, (wide, wide), 1)
    slabs = wide // tall
    for part in range(deep * tall // wide):
        t = heat[slabs * part : slabs * (part + 1)].reshape(wide, wide)
        m = blend[slabs * part : slabs * (part + 1)].reshape(wide, wide)
        ends = jnp.where(lane == 0, t, pltpu.roll(t, 2, 1))
        more = jnp.where(lane == 2, pltpu.roll(m, 2, 1), pltpu.roll(m, 4, 1))
        turned = jnp.where(lane < 2, ends, more).T
        here = slice(wide * part, wide * (part + 1))
        x_lo[0:1, here] = turned[0:1]
        x_hi[0:1, here] = turned[1:2]
        x_lo[1:2, here] = turned[2:3]
        x_hi[1:2, here] = turned[3:4]


def faces(heat, blend):
    deep, tall, wide = heat.shape
    shapes = [(2, deep * tall)] * 2 + [(2, deep, wide)] * 2 + [(2, tall, wide)] * 2
    return pl.pallas_call(
        face_kernel,
        out_shape=[jax.ShapeDtypeStruct(s, F32) for s in shapes],
        compiler_params=SMALL,
        name="faces",
    )(heat, blend)


def split3(values):
    high = values.astype(jnp.bfloat16).astype(F32)
    rest = values - high
    middle = rest.astype(jnp.bfloat16).astype(F32)
    return [high, middle, rest - middle]


def brick_kernel(
    spacing, order, weights, light, heat, blend, filled, x_lo, x_hi, y_lo, y_hi, z_lo, z_hi,
    x_own_lo, x_own_hi, image, x_step, veil,
):
    deep, tall, wide = heat.shape
    at = []
    for axis in ("gx", "gy", "gz"):
        at += [lax.axis_index(axis) == 0, lax.axis_index(axis) == lax.axis_size(axis) - 1]
    below = jnp.where(at[0], x_own_lo[...], x_lo[...])
    above = jnp.where(at[1], x_own_hi[...], x_hi[...])
    sides = jnp.concatenate([below, above, jnp.zeros((4, deep * tall), F32)], axis=0)
    sides = jnp.concatenate(split3(sides) + [jnp.zeros_like(sides)], axis=0).astype(jnp.bfloat16)
    row = lax.broadcasted_iota(jnp.int32, (32, 2 * wide), 0)
    side = row % 8
    column = lax.broadcasted_iota(jnp.int32, (32, 2 * wide), 1)
    spread = jnp.where(
        (side < 2) & (column == side * wide), -1.0,
        jnp.where((side >= 2) & (side < 4) & (column == (side - 2) * wide + wide - 1), 1.0, 0.0),
    ).astype(jnp.bfloat16)
    across = (((0,), (0,)), ((), ()))
    x_step[...] = lax.dot_general(sides, spread, across, preferred_element_type=F32)
    slab = lax.broadcasted_iota(jnp.int32, (deep, deep * wide), 0)
    column = lax.broadcasted_iota(jnp.int32, (deep, deep * wide), 1)
    same = (column // wide == slab).astype(F32)
    veil[...] = lax.dot_general(
        filled[...].astype(F32), same, across, preferred_element_type=F32
    ) * (-spacing)
    half = [0.5, 0.5, 0.5, 1.0]
    w = [[weights[r, k] * half[r] for k in range(7)] for r in range(4)]
    base = [w[r][6] + w[r][2] + w[r][3] for r in range(4)]
    sun = [light[i] * 0.5 for i in range(3)]
    fields = (heat, blend)
    lane8 = lax.broadcasted_iota(jnp.int32, (8, wide), 1)
    not_first = lane8 > 0
    not_last = lane8 < wide - 1
    for block in range(tall // 8):
        top = 8 * block
        rows = slice(top, top + 8)
        through = jnp.ones((8, wide), F32)
        sums = [jnp.zeros((8, wide), F32) for _ in range(4)]

        def cells(index, z):
            if z < 0:
                return jnp.where(at[4], fields[index][0, rows, :], z_lo[index, rows, :])
            if z == deep:
                return jnp.where(at[5], fields[index][deep - 1, rows, :], z_hi[index, rows, :])
            return fields[index][z, rows, :]

        for z in range(deep):
            slopes = []
            for index in range(2):
                field = fields[index]
                here = field[z, rows, :]
                dz = cells(index, z + 1) - cells(index, z - 1)
                if block == 0:
                    edge = jnp.where(at[2], field[z, 0:1, :], y_lo[index, z : z + 1, :])
                    up = jnp.concatenate([edge, field[z, 0:7, :]], axis=0)
                else:
                    up = field[z, top - 1 : top + 7, :]
                if top + 8 == tall:
                    edge = jnp.where(at[3], field[z, tall - 1 : tall, :], y_hi[index, z : z + 1, :])
                    down = jnp.concatenate([field[z, top + 1 : tall, :], edge], axis=0)
                else:
                    down = field[z, top + 1 : top + 9, :]
                dy = down - up
                right = jnp.where(not_last, pltpu.roll(here, wide - 1, 1), 0.0)
                left = jnp.where(not_first, pltpu.roll(here, 1, 1), 0.0)
                outer = x_step[z * tall + top : z * tall + top + 8, index * wide : (index + 1) * wide]
                dx = right - left + outer
                slopes.append((here, dz, dy, dx))
            t, tz, ty, tx = slopes[0]
            m, mz, my, mx = slopes[1]
            t_sq = tz * tz + ty * ty + tx * tx
            m_sq = mz * mz + my * my + mx * mx
            t_inverse = lax.rsqrt(t_sq * 0.25 + 1.0)
            m_inverse = lax.rsqrt(m_sq * 0.25 + 1.0)
            t_rest = t_inverse * t_inverse
            m_rest = m_inverse * m_inverse
            lit = (tx * sun[0] + ty * sun[1] + tz * sun[2]) * t_inverse
            both = t * m
            linear = [
                (base[r] + w[r][0] * t)
                + (w[r][1] * m + w[r][5] * both)
                + (w[r][4] * lit - (w[r][2] * t_rest + w[r][3] * m_rest))
                for r in range(4)
            ]
            soft = jnp.maximum(linear[3], 0.0) + jnp.log(1.0 + jnp.exp(-jnp.abs(linear[3])))
            kept = jnp.exp(soft * veil[rows, z * wide : (z + 1) * wide])
            weight = (1.0 - kept) * through
            through = through * kept
            for r in range(3):
                sums[r] = sums[r] + weight * jnp.tanh(linear[r])
            sums[3] = sums[3] + weight
        for r in range(3):
            sums[r] = 0.5 * (sums[r] + sums[3])
        for j in range(4):
            for r in range(4):
                image[order[4 * block + j], 2 * r : 2 * r + 2, :] = sums[r][2 * j : 2 * j + 2]


def over_kernel(order, parts, frame):
    wide = parts.shape[2]
    row = lax.broadcasted_iota(jnp.int32, (8, wide), 0)
    through = jnp.ones((8, wide), F32)
    total = jnp.zeros((8, wide), F32)
    for z in range(parts.shape[0]):
        part = parts[order[z]]
        veil = jnp.where(row >= 6, part, 0.0)
        veil = veil + pltpu.roll(veil, 4, 0)
        veil = veil + pltpu.roll(veil, 2, 0)
        total = total + through * part
        through = through * (1.0 - veil)
    for r in range(4):
        frame[r] = total[2 * r : 2 * r + 2]


def on_device(heat, blend, filled, weights, light):
    deep, tall, wide = heat.shape
    depth_count = lax.axis_size("gz")
    spacing = 2.0 / (deep * depth_count)
    own = faces(heat, blend)
    halos = []
    for axis, lo, hi in (("gx", own[0], own[1]), ("gy", own[2], own[3]), ("gz", own[4], own[5])):
        count = lax.axis_size(axis)
        halos.append(lax.ppermute(hi, axis, [(i, i + 1) for i in range(count - 1)]))
        halos.append(lax.ppermute(lo, axis, [(i + 1, i) for i in range(count - 1)]))
    first = depth_count * 5 // 8
    group = [(first + i) % depth_count for i in range(depth_count)]
    order = [group.index(z) for z in range(depth_count)]
    smem = pl.BlockSpec(memory_space=pltpu.SMEM)
    vmem = pl.BlockSpec(memory_space=pltpu.VMEM)

    def brick(*refs):
        brick_kernel(spacing, order, *refs)

    def over(*refs):
        over_kernel(order, *refs)

    image = pl.pallas_call(
        brick,
        out_shape=jax.ShapeDtypeStruct((depth_count, 8, wide), F32),
        in_specs=[smem] * 2 + [vmem] * 11,
        scratch_shapes=[
            pltpu.VMEM((deep * tall, 2 * wide), F32),
            pltpu.VMEM((tall, deep * wide), F32),
        ],
        compiler_params=SMALL,
        name="brick",
    )(weights, light, heat, blend, filled.reshape(deep, tall), *halos, own[0], own[1])
    parts = lax.all_to_all(image, "gz", 0, 0, tiled=True, axis_index_groups=[group])
    return pl.pallas_call(
        over,
        out_shape=jax.ShapeDtypeStruct((4, tall // depth_count, wide), F32),
        compiler_params=SMALL,
        name="over",
    )(parts)


def solution(mesh):
    placed = (P("gz", "gy", "gx"), P("gz", "gy", "gx"), P("gz", "gy", "gx"), P(), P())
    return jax.shard_map(
        on_device,
        mesh=mesh,
        in_specs=placed,
        out_specs=P(None, ("gy", "gz"), "gx"),
        check_vma=False,
    )
```

```python
import jax
import jax.numpy as jnp
from jax import lax
from jax.experimental import pallas as pl
from jax.experimental.pallas import tpu as pltpu
from jax.sharding import PartitionSpec as P

F32 = jnp.float32
SMALL = pltpu.CompilerParams(vmem_limit_bytes=8 * 2**20)


def odd_place(axis):
    return lax.axis_index(axis) % 2 == 1


def face_kernel(far_heat, far_blend, heat, blend, x_a, x_b, y_a, y_b, z_a, z_b, arrived):
    deep, tall, wide = heat.shape
    halves = [slice(0, deep // 2), slice(deep // 2, deep)]
    copies = [
        [
            pltpu.make_async_copy(far.at[half], near.at[half], arrived.at[2 * h + f])
            for f, (far, near) in enumerate(((far_heat, heat), (far_blend, blend)))
        ]
        for h, half in enumerate(halves)
    ]
    for pair in copies:
        for copy in pair:
            copy.start()
    odd_x, odd_y, odd_z = [odd_place(axis) for axis in ("gx", "gy", "gz")]
    lane = lax.broadcasted_iota(jnp.int32, (wide, wide), 1)
    slabs = wide // tall
    parts = deep * tall // wide
    for part in range(parts):
        if part % (parts // 2) == 0:
            for copy in copies[part // (parts // 2)]:
                copy.wait()
        t = heat[slabs * part : slabs * (part + 1)].reshape(wide, wide)
        m = blend[slabs * part : slabs * (part + 1)].reshape(wide, wide)
        ends = jnp.where(lane == 0, t, pltpu.roll(t, 2, 1))
        more = jnp.where(lane == 2, pltpu.roll(m, 2, 1), pltpu.roll(m, 4, 1))
        turned = jnp.where(lane < 2, ends, more).T
        here = slice(wide * part, wide * (part + 1))
        for f in range(2):
            low, high = turned[2 * f : 2 * f + 1], turned[2 * f + 1 : 2 * f + 2]
            x_a[f : f + 1, here] = jnp.where(odd_x, low, high)
            x_b[f : f + 1, here] = jnp.where(odd_x, high, low)
    for f, field in enumerate((heat, blend)):
        low, high = field[0], field[deep - 1]
        z_a[f] = jnp.where(odd_z, low, high)
        z_b[f] = jnp.where(odd_z, high, low)
        low = jnp.concatenate([field[z, 0:1, :] for z in range(deep)], axis=0)
        high = jnp.concatenate([field[z, tall - 1 : tall, :] for z in range(deep)], axis=0)
        y_a[f] = jnp.where(odd_y, low, high)
        y_b[f] = jnp.where(odd_y, high, low)


def faces(heat, blend):
    deep, tall, wide = heat.shape
    shapes = [heat.shape] * 2
    shapes += [(2, deep * tall)] * 2 + [(2, deep, wide)] * 2 + [(2, tall, wide)] * 2
    return pl.pallas_call(
        face_kernel,
        out_shape=[jax.ShapeDtypeStruct(s, F32) for s in shapes],
        in_specs=[pl.BlockSpec(memory_space=pltpu.HBM)] * 2,
        scratch_shapes=[pltpu.SemaphoreType.DMA((4,))],
        compiler_params=SMALL,
        name="faces",
    )(pltpu.with_memory_space_constraint(heat, pltpu.HBM), pltpu.with_memory_space_constraint(blend, pltpu.HBM))


def split3(values):
    high = values.astype(jnp.bfloat16).astype(F32)
    rest = values - high
    middle = rest.astype(jnp.bfloat16).astype(F32)
    return [high, middle, rest - middle]


def brick_kernel(
    spacing, order, weights, light, heat, blend, filled, x_a, x_b, y_a, y_b, z_a, z_b,
    x_own_b, image, x_step, veil,
):
    deep, tall, wide = heat.shape
    at = []
    for axis in ("gx", "gy", "gz"):
        at += [lax.axis_index(axis) == 0, lax.axis_index(axis) == lax.axis_size(axis) - 1]
    odd_x, odd_y, odd_z = [odd_place(axis) for axis in ("gx", "gy", "gz")]
    first = jnp.where(at[0], x_own_b[...], jnp.where(odd_x, x_a[...], x_b[...]))
    last = jnp.where(at[1], x_own_b[...], jnp.where(odd_x, x_b[...], x_a[...]))
    sides = jnp.concatenate([first, last, jnp.zeros((4, deep * tall), F32)], axis=0)
    sides = jnp.concatenate(split3(sides) + [jnp.zeros_like(sides)], axis=0).astype(jnp.bfloat16)
    row = lax.broadcasted_iota(jnp.int32, (32, 2 * wide), 0)
    side = row % 8
    column = lax.broadcasted_iota(jnp.int32, (32, 2 * wide), 1)
    spread = jnp.where(
        (side < 2) & (column == side * wide), -1.0,
        jnp.where((side >= 2) & (side < 4) & (column == (side - 2) * wide + wide - 1), 1.0, 0.0),
    ).astype(jnp.bfloat16)
    across = (((0,), (0,)), ((), ()))
    x_step[...] = lax.dot_general(sides, spread, across, preferred_element_type=F32)
    slab = lax.broadcasted_iota(jnp.int32, (deep, deep * wide), 0)
    column = lax.broadcasted_iota(jnp.int32, (deep, deep * wide), 1)
    same = (column // wide == slab).astype(F32)
    veil[...] = lax.dot_general(
        filled[...].astype(F32), same, across, preferred_element_type=F32
    ) * (-spacing)
    half = [0.5, 0.5, 0.5, 1.0]
    w = [[weights[r, k] * half[r] for k in range(7)] for r in range(4)]
    base = [w[r][6] + w[r][2] + w[r][3] for r in range(4)]
    sun = [light[i] * 0.5 for i in range(3)]
    fields = (heat, blend)
    lane8 = lax.broadcasted_iota(jnp.int32, (8, wide), 1)
    not_first = lane8 > 0
    not_last = lane8 < wide - 1
    for block in range(tall // 8):
        top = 8 * block
        rows = slice(top, top + 8)
        through = jnp.ones((8, wide), F32)
        sums = [jnp.zeros((8, wide), F32) for _ in range(4)]

        def cells(index, z):
            if z < 0:
                other = jnp.where(odd_z, z_a[index, rows, :], z_b[index, rows, :])
                return jnp.where(at[4], fields[index][0, rows, :], other)
            if z == deep:
                other = jnp.where(odd_z, z_b[index, rows, :], z_a[index, rows, :])
                return jnp.where(at[5], fields[index][deep - 1, rows, :], other)
            return fields[index][z, rows, :]

        for z in range(deep):
            slopes = []
            for index in range(2):
                field = fields[index]
                here = field[z, rows, :]
                dz = cells(index, z + 1) - cells(index, z - 1)
                if block == 0:
                    edge = jnp.where(odd_y, y_a[index, z : z + 1, :], y_b[index, z : z + 1, :])
                    edge = jnp.where(at[2], field[z, 0:1, :], edge)
                    up = jnp.concatenate([edge, field[z, 0:7, :]], axis=0)
                else:
                    up = field[z, top - 1 : top + 7, :]
                if top + 8 == tall:
                    edge = jnp.where(odd_y, y_b[index, z : z + 1, :], y_a[index, z : z + 1, :])
                    edge = jnp.where(at[3], field[z, tall - 1 : tall, :], edge)
                    down = jnp.concatenate([field[z, top + 1 : tall, :], edge], axis=0)
                else:
                    down = field[z, top + 1 : top + 9, :]
                dy = down - up
                right = jnp.where(not_last, pltpu.roll(here, wide - 1, 1), 0.0)
                left = jnp.where(not_first, pltpu.roll(here, 1, 1), 0.0)
                outer = x_step[z * tall + top : z * tall + top + 8, index * wide : (index + 1) * wide]
                dx = right - left + outer
                slopes.append((here, dz, dy, dx))
            t, tz, ty, tx = slopes[0]
            m, mz, my, mx = slopes[1]
            t_sq = tz * tz + ty * ty + tx * tx
            m_sq = mz * mz + my * my + mx * mx
            t_inverse = lax.rsqrt(t_sq * 0.25 + 1.0)
            m_inverse = lax.rsqrt(m_sq * 0.25 + 1.0)
            t_rest = t_inverse * t_inverse
            m_rest = m_inverse * m_inverse
            lit = (tx * sun[0] + ty * sun[1] + tz * sun[2]) * t_inverse
            both = t * m
            linear = [
                (base[r] + w[r][0] * t)
                + (w[r][1] * m + w[r][5] * both)
                + (w[r][4] * lit - (w[r][2] * t_rest + w[r][3] * m_rest))
                for r in range(4)
            ]
            soft = jnp.maximum(linear[3], 0.0) + jnp.log(1.0 + jnp.exp(-jnp.abs(linear[3])))
            kept = jnp.exp(soft * veil[rows, z * wide : (z + 1) * wide])
            weight = (1.0 - kept) * through
            through = through * kept
            for r in range(3):
                sums[r] = sums[r] + weight * jnp.tanh(linear[r])
            sums[3] = sums[3] + weight
        for r in range(3):
            sums[r] = 0.5 * (sums[r] + sums[3])
        for j in range(4):
            for r in range(4):
                image[order[4 * block + j], 2 * r : 2 * r + 2, :] = sums[r][2 * j : 2 * j + 2]


def over_kernel(order, parts, frame):
    wide = parts.shape[2]
    row = lax.broadcasted_iota(jnp.int32, (8, wide), 0)
    through = jnp.ones((8, wide), F32)
    total = jnp.zeros((8, wide), F32)
    for z in range(parts.shape[0]):
        part = parts[order[z]]
        veil = jnp.where(row >= 6, part, 0.0)
        veil = veil + pltpu.roll(veil, 4, 0)
        veil = veil + pltpu.roll(veil, 2, 0)
        total = total + through * part
        through = through * (1.0 - veil)
    for r in range(4):
        frame[r] = total[2 * r : 2 * r + 2]


def on_device(heat, blend, filled, weights, light):
    deep, tall, wide = heat.shape
    depth_count = lax.axis_size("gz")
    spacing = 2.0 / (deep * depth_count)
    heat, blend, *own = faces(heat, blend)
    halos = []
    for axis, a, b in (("gx", own[0], own[1]), ("gy", own[2], own[3]), ("gz", own[4], own[5])):
        count = lax.axis_size(axis)
        halos.append(lax.ppermute(a, axis, [(i, i ^ 1) for i in range(count)]))
        halos.append(lax.ppermute(b, axis, [(i, ((i + 1) ^ 1) - 1) for i in range(1, count - 1)]))
    first = depth_count * 5 // 8
    group = [(first + i) % depth_count for i in range(depth_count)]
    order = [group.index(z) for z in range(depth_count)]
    smem = pl.BlockSpec(memory_space=pltpu.SMEM)
    vmem = pl.BlockSpec(memory_space=pltpu.VMEM)

    def brick(*refs):
        brick_kernel(spacing, order, *refs)

    def over(*refs):
        over_kernel(order, *refs)

    image = pl.pallas_call(
        brick,
        out_shape=jax.ShapeDtypeStruct((depth_count, 8, wide), F32),
        in_specs=[smem] * 2 + [vmem] * 10,
        scratch_shapes=[
            pltpu.VMEM((deep * tall, 2 * wide), F32),
            pltpu.VMEM((tall, deep * wide), F32),
        ],
        compiler_params=SMALL,
        name="brick",
    )(weights, light, heat, blend, filled.reshape(deep, tall), *halos, own[1])
    parts = lax.all_to_all(image, "gz", 0, 0, tiled=True, axis_index_groups=[group])
    return pl.pallas_call(
        over,
        out_shape=jax.ShapeDtypeStruct((4, tall // depth_count, wide), F32),
        compiler_params=SMALL,
        name="over",
    )(parts)


def solution(mesh):
    placed = (P("gz", "gy", "gx"), P("gz", "gy", "gx"), P("gz", "gy", "gx"), P(), P())
    return jax.shard_map(
        on_device,
        mesh=mesh,
        in_specs=placed,
        out_specs=P(None, ("gy", "gz"), "gx"),
        check_vma=False,
    )
```

```python
import jax
import jax.numpy as jnp
from jax import lax
from jax.experimental import pallas as pl
from jax.experimental.pallas import tpu as pltpu
from jax.sharding import PartitionSpec as P

F32 = jnp.float32
SMALL = pltpu.CompilerParams(vmem_limit_bytes=8 * 2**20)


def in_hbm(array):
    return pltpu.with_memory_space_constraint(array, pltpu.HBM)


def odd_place(axis):
    return lax.axis_index(axis) % 2 == 1


def seat(column, core, columns):
    return lax.rem(column + columns - 1, columns) * 2 + 1 - core


def seats(columns, rows):
    return [
        [(i + 1) % columns * rows + 2 * chip + core for i in range(columns) for core in (1, 0)]
        for chip in range(rows // 2)
    ]


def face_kernel(
    far_heat, far_blend, heat, blend, flat, x_own, y_b, z_a, z_b, x_faces, arrived
):
    deep, tall, wide = heat.shape
    halves = [slice(0, deep // 2), slice(deep // 2, deep)]
    copies = [
        [
            pltpu.make_async_copy(far.at[half], near.at[half], arrived.at[2 * h + f])
            for f, (far, near) in enumerate(((far_heat, heat), (far_blend, blend)))
        ]
        for h, half in enumerate(halves)
    ]
    for pair in copies:
        for copy in pair:
            copy.start()
    x_faces[...] = jnp.zeros_like(x_faces)
    odd_y, odd_z = odd_place("gy"), odd_place("gz")
    lane = lax.broadcasted_iota(jnp.int32, (wide, wide), 1)
    slabs = wide // tall
    parts = deep * tall // wide
    for part in range(parts):
        if part % (parts // 2) == 0:
            for copy in copies[part // (parts // 2)]:
                copy.wait()
        t = heat[slabs * part : slabs * (part + 1)].reshape(wide, wide)
        m = blend[slabs * part : slabs * (part + 1)].reshape(wide, wide)
        ends = jnp.where(lane == 0, t, pltpu.roll(t, 2, 1))
        more = jnp.where(lane == 2, pltpu.roll(m, 2, 1), pltpu.roll(m, 4, 1))
        turned = jnp.where(lane < 2, ends, more).T
        for f in range(2):
            for side in range(2):
                at = 2 * f + side
                x_faces[side, f, part : part + 1, :] = turned[at : at + 1]
    column, columns = lax.axis_index("gx"), lax.axis_size("gx")
    core = lax.axis_index("gy") % 2
    for f, field in enumerate((heat, blend)):
        low, high = field[0], field[deep - 1]
        z_a[f] = jnp.where(odd_z, low, high)
        z_b[f] = jnp.where(odd_z, high, low)
        low = jnp.concatenate([field[z, 0:1, :] for z in range(deep)], axis=0)
        high = jnp.concatenate([field[z, tall - 1 : tall, :] for z in range(deep)], axis=0)
        y_b[f] = jnp.where(odd_y, high, low)
        beside = jnp.where(odd_y, low, high)
        left, right = x_faces[0, f], x_faces[1, f]
        x_own[f] = jnp.where(column == 0, left, right)
        for i in range(columns):
            other = (i + 1) % columns
            along = jnp.where(column < other, right, left)
            for place, its in ((2 * i, 1), (2 * i + 1, 0)):
                flat[place, f] = jnp.where(core == its, along, beside)


def faces(heat, blend):
    deep, tall, wide = heat.shape
    members = 2 * lax.axis_size("gx")
    shapes = [heat.shape] * 2 + [(members, 2, deep, wide)] + [(2, deep, wide)] * 2
    shapes += [(2, tall, wide)] * 2
    return pl.pallas_call(
        face_kernel,
        out_shape=[jax.ShapeDtypeStruct(s, F32) for s in shapes],
        in_specs=[pl.BlockSpec(memory_space=pltpu.HBM)] * 2,
        scratch_shapes=[pltpu.VMEM((2, 2, deep, wide), F32), pltpu.SemaphoreType.DMA((4,))],
        compiler_params=SMALL,
        name="faces",
    )(in_hbm(heat), in_hbm(blend))


def split3(values):
    high = values.astype(jnp.bfloat16).astype(F32)
    rest = values - high
    middle = rest.astype(jnp.bfloat16).astype(F32)
    return [high, middle, rest - middle]


def brick_kernel(
    spacing, order, far_weights, far_light, heat, blend, filled, flat, x_own, y_b, z_a, z_b,
    image, x_step, veil, weights, light, arrived,
):
    deep, tall, wide = heat.shape
    copies = [
        pltpu.make_async_copy(far_weights, weights, arrived.at[0]),
        pltpu.make_async_copy(far_light, light, arrived.at[1]),
    ]
    for copy in copies:
        copy.start()
    at = []
    for axis in ("gx", "gy", "gz"):
        at += [lax.axis_index(axis) == 0, lax.axis_index(axis) == lax.axis_size(axis) - 1]
    odd_y, odd_z = odd_place("gy"), odd_place("gz")
    column, columns = lax.axis_index("gx"), lax.axis_size("gx")
    core = lax.axis_index("gy") % 2
    left = seat(lax.rem(column + columns - 1, columns), core, columns)
    right = seat(lax.rem(column + 1, columns), core, columns)
    y_a = flat.at[seat(column, 1 - core, columns)]
    parts = deep * tall // wide
    sides = []
    for edge, place in ((at[0], left), (at[1], right)):
        for f in range(2):
            face = jnp.where(edge, x_own[f], flat[place, f])
            sides.append(jnp.concatenate([face[p : p + 1] for p in range(parts)], axis=1))
    sides = jnp.concatenate(sides + [jnp.zeros((4, deep * tall), F32)], axis=0)
    sides = jnp.concatenate(split3(sides) + [jnp.zeros_like(sides)], axis=0).astype(jnp.bfloat16)
    row = lax.broadcasted_iota(jnp.int32, (32, 2 * wide), 0)
    side = row % 8
    column = lax.broadcasted_iota(jnp.int32, (32, 2 * wide), 1)
    spread = jnp.where(
        (side < 2) & (column == side * wide), -1.0,
        jnp.where((side >= 2) & (side < 4) & (column == (side - 2) * wide + wide - 1), 1.0, 0.0),
    ).astype(jnp.bfloat16)
    across = (((0,), (0,)), ((), ()))
    x_step[...] = lax.dot_general(sides, spread, across, preferred_element_type=F32)
    slab = lax.broadcasted_iota(jnp.int32, (deep, deep * wide), 0)
    column = lax.broadcasted_iota(jnp.int32, (deep, deep * wide), 1)
    same = (column // wide == slab).astype(F32)
    veil[...] = lax.dot_general(
        filled[...].astype(F32), same, across, preferred_element_type=F32
    ) * (-spacing)
    for copy in copies:
        copy.wait()
    half = [0.5, 0.5, 0.5, 1.0]
    w = [[weights[r, k] * half[r] for k in range(7)] for r in range(4)]
    base = [w[r][6] + w[r][2] + w[r][3] for r in range(4)]
    sun = [light[i] * 0.5 for i in range(3)]
    fields = (heat, blend)
    lane8 = lax.broadcasted_iota(jnp.int32, (8, wide), 1)
    not_first = lane8 > 0
    not_last = lane8 < wide - 1
    for block in range(tall // 8):
        top = 8 * block
        rows = slice(top, top + 8)
        through = jnp.ones((8, wide), F32)
        sums = [jnp.zeros((8, wide), F32) for _ in range(4)]

        def cells(index, z):
            if z < 0:
                other = jnp.where(odd_z, z_a[index, rows, :], z_b[index, rows, :])
                return jnp.where(at[4], fields[index][0, rows, :], other)
            if z == deep:
                other = jnp.where(odd_z, z_b[index, rows, :], z_a[index, rows, :])
                return jnp.where(at[5], fields[index][deep - 1, rows, :], other)
            return fields[index][z, rows, :]

        for z in range(deep):
            slopes = []
            for index in range(2):
                field = fields[index]
                here = field[z, rows, :]
                dz = cells(index, z + 1) - cells(index, z - 1)
                if block == 0:
                    edge = jnp.where(odd_y, y_a[index, z : z + 1, :], y_b[index, z : z + 1, :])
                    edge = jnp.where(at[2], field[z, 0:1, :], edge)
                    up = jnp.concatenate([edge, field[z, 0:7, :]], axis=0)
                else:
                    up = field[z, top - 1 : top + 7, :]
                if top + 8 == tall:
                    edge = jnp.where(odd_y, y_b[index, z : z + 1, :], y_a[index, z : z + 1, :])
                    edge = jnp.where(at[3], field[z, tall - 1 : tall, :], edge)
                    down = jnp.concatenate([field[z, top + 1 : tall, :], edge], axis=0)
                else:
                    down = field[z, top + 1 : top + 9, :]
                dy = down - up
                right = jnp.where(not_last, pltpu.roll(here, wide - 1, 1), 0.0)
                left = jnp.where(not_first, pltpu.roll(here, 1, 1), 0.0)
                outer = x_step[z * tall + top : z * tall + top + 8, index * wide : (index + 1) * wide]
                dx = right - left + outer
                slopes.append((here, dz, dy, dx))
            t, tz, ty, tx = slopes[0]
            m, mz, my, mx = slopes[1]
            t_sq = tz * tz + ty * ty + tx * tx
            m_sq = mz * mz + my * my + mx * mx
            t_inverse = lax.rsqrt(t_sq * 0.25 + 1.0)
            m_inverse = lax.rsqrt(m_sq * 0.25 + 1.0)
            t_rest = t_inverse * t_inverse
            m_rest = m_inverse * m_inverse
            lit = (tx * sun[0] + ty * sun[1] + tz * sun[2]) * t_inverse
            both = t * m
            linear = [
                (base[r] + w[r][0] * t)
                + (w[r][1] * m + w[r][5] * both)
                + (w[r][4] * lit - (w[r][2] * t_rest + w[r][3] * m_rest))
                for r in range(4)
            ]
            soft = jnp.maximum(linear[3], 0.0) + jnp.log(1.0 + jnp.exp(-jnp.abs(linear[3])))
            kept = jnp.exp(soft * veil[rows, z * wide : (z + 1) * wide])
            weight = (1.0 - kept) * through
            through = through * kept
            for r in range(3):
                sums[r] = sums[r] + weight * jnp.tanh(linear[r])
            sums[3] = sums[3] + weight
        for r in range(3):
            sums[r] = 0.5 * (sums[r] + sums[3])
        for j in range(4):
            for r in range(4):
                image[order[4 * block + j], 2 * r : 2 * r + 2, :] = sums[r][2 * j : 2 * j + 2]


def over_kernel(order, parts, out):
    count, rows, wide = parts.shape
    row = lax.broadcasted_iota(jnp.int32, (8, wide), 0)
    for top in range(0, rows, 8):
        through = jnp.ones((8, wide), F32)
        total = jnp.zeros((8, wide), F32)
        for i in range(count):
            part = parts[order[i], top : top + 8, :]
            veil = jnp.where(row >= 6, part, 0.0)
            veil = veil + pltpu.roll(veil, 4, 0)
            veil = veil + pltpu.roll(veil, 2, 0)
            total = total + through * part
            through = through * (1.0 - veil)
        if out.shape[0] == 4:
            for r in range(4):
                out[r] = total[2 * r : 2 * r + 2]
        else:
            out[top : top + 8, :] = total


def over(parts, order, shape):
    def kernel(*refs):
        over_kernel(order, *refs)

    return pl.pallas_call(
        kernel, out_shape=jax.ShapeDtypeStruct(shape, F32), compiler_params=SMALL, name="over"
    )(parts)


def on_device(heat, blend, filled, weights, light):
    deep, tall, wide = heat.shape
    depth_count = lax.axis_size("gz")
    spacing = 2.0 / (deep * depth_count)
    heat, blend, flat, x_own, y_b, z_a, z_b = faces(heat, blend)
    flat = lax.all_to_all(
        flat, ("gx", "gy"), 0, 0, tiled=True,
        axis_index_groups=seats(lax.axis_size("gx"), lax.axis_size("gy")),
    )
    swap = {
        axis: [(i, ((i + 1) ^ 1) - 1) for i in range(1, lax.axis_size(axis) - 1)]
        for axis in ("gy", "gz")
    }
    y_b = lax.ppermute(y_b, "gy", swap["gy"])
    z_a = lax.ppermute(z_a, "gz", [(i, i ^ 1) for i in range(depth_count)])
    z_b = lax.ppermute(z_b, "gz", swap["gz"])
    near = 4
    far = depth_count // near
    turn = [(far // 2 + i) % far for i in range(far)]
    far_order = [turn.index(i) for i in range(far)]
    near_groups = [[near * i + k for k in range(near)] for i in range(far)]
    far_groups = [[near * i + k for i in turn] for k in range(near)]
    order = [(z % near) * far + far_order[z // near] for z in range(depth_count)]
    hbm = pl.BlockSpec(memory_space=pltpu.HBM)
    vmem = pl.BlockSpec(memory_space=pltpu.VMEM)

    def brick(*refs):
        brick_kernel(spacing, order, *refs)

    image = pl.pallas_call(
        brick,
        out_shape=jax.ShapeDtypeStruct((depth_count, 8, wide), F32),
        in_specs=[hbm] * 2 + [vmem] * 8,
        scratch_shapes=[
            pltpu.VMEM((deep * tall, 2 * wide), F32),
            pltpu.VMEM((tall, deep * wide), F32),
            pltpu.SMEM(weights.shape, F32),
            pltpu.SMEM(light.shape, F32),
            pltpu.SemaphoreType.DMA((2,)),
        ],
        compiler_params=SMALL,
        name="brick",
    )(in_hbm(weights), in_hbm(light), heat, blend, filled.reshape(deep, tall), flat, x_own, y_b, z_a, z_b)
    parts = lax.all_to_all(image, "gz", 0, 0, tiled=True, axis_index_groups=near_groups)
    joined = over(parts.reshape(near, far * 8, wide), list(range(near)), (far * 8, wide))
    parts = lax.all_to_all(
        joined.reshape(far, 8, wide), "gz", 0, 0, tiled=True, axis_index_groups=far_groups
    )
    return over(parts, far_order, (4, tall // depth_count, wide))


def solution(mesh):
    placed = (P("gz", "gy", "gx"), P("gz", "gy", "gx"), P("gz", "gy", "gx"), P(), P())
    return jax.shard_map(
        on_device,
        mesh=mesh,
        in_specs=placed,
        out_specs=P(None, ("gy", "gz"), "gx"),
        check_vma=False,
    )
```

```python
import jax
import jax.numpy as jnp
from jax import lax
from jax.experimental import pallas as pl
from jax.experimental.pallas import tpu as pltpu
from jax.sharding import PartitionSpec as P

F32 = jnp.float32
SMALL = pltpu.CompilerParams(vmem_limit_bytes=8 * 2**20)


def in_hbm(array):
    return pltpu.with_memory_space_constraint(array, pltpu.HBM)


def odd_place(axis):
    return lax.axis_index(axis) % 2 == 1


def seat(column, core, columns):
    return lax.rem(column + columns - 1, columns) * 2 + 1 - core


def seats(columns, rows):
    return [
        [(i + 1) % columns * rows + 2 * chip + core for i in range(columns) for core in (1, 0)]
        for chip in range(rows // 2)
    ]


def face_kernel(
    far_heat, far_blend, heat, blend, flat, x_own, y_b, z_a, z_b, x_faces, arrived
):
    deep, tall, wide = heat.shape
    halves = [slice(0, deep // 2), slice(deep // 2, deep)]
    copies = [
        [
            pltpu.make_async_copy(far.at[half], near.at[half], arrived.at[2 * h + f])
            for f, (far, near) in enumerate(((far_heat, heat), (far_blend, blend)))
        ]
        for h, half in enumerate(halves)
    ]
    for pair in copies:
        for copy in pair:
            copy.start()
    x_faces[...] = jnp.zeros_like(x_faces)
    odd_y, odd_z = odd_place("gy"), odd_place("gz")
    lane = lax.broadcasted_iota(jnp.int32, (wide, wide), 1)
    slabs = wide // tall
    parts = deep * tall // wide
    for part in range(parts):
        if part % (parts // 2) == 0:
            for copy in copies[part // (parts // 2)]:
                copy.wait()
        t = heat[slabs * part : slabs * (part + 1)].reshape(wide, wide)
        m = blend[slabs * part : slabs * (part + 1)].reshape(wide, wide)
        ends = jnp.where(lane == 0, t, pltpu.roll(t, 2, 1))
        more = jnp.where(lane == 2, pltpu.roll(m, 2, 1), pltpu.roll(m, 4, 1))
        turned = jnp.where(lane < 2, ends, more).T
        for f in range(2):
            for side in range(2):
                at = 2 * f + side
                x_faces[side, f, part : part + 1, :] = turned[at : at + 1]
    column, columns = lax.axis_index("gx"), lax.axis_size("gx")
    core = lax.axis_index("gy") % 2
    for f, field in enumerate((heat, blend)):
        low, high = field[0], field[deep - 1]
        z_a[f] = jnp.where(odd_z, low, high)
        z_b[f] = jnp.where(odd_z, high, low)
        low = jnp.concatenate([field[z, 0:1, :] for z in range(deep)], axis=0)
        high = jnp.concatenate([field[z, tall - 1 : tall, :] for z in range(deep)], axis=0)
        y_b[f] = jnp.where(odd_y, high, low)
        beside = jnp.where(odd_y, low, high)
        left, right = x_faces[0, f], x_faces[1, f]
        x_own[f] = jnp.where(column == 0, left, right)
        for i in range(columns):
            other = (i + 1) % columns
            along = jnp.where(column < other, right, left)
            for place, its in ((2 * i, 1), (2 * i + 1, 0)):
                flat[place, f, 0:deep, :] = jnp.where(core == its, along, beside)
                flat[place, f, deep:, :] = jnp.zeros((deep, wide), F32)


def faces(heat, blend):
    deep, tall, wide = heat.shape
    members = 2 * lax.axis_size("gx")
    shapes = [heat.shape] * 2 + [(members, 2, 2 * deep, wide)] + [(2, deep, wide)] * 2
    shapes += [(2, tall, wide)] * 2
    return pl.pallas_call(
        face_kernel,
        out_shape=[jax.ShapeDtypeStruct(s, F32) for s in shapes],
        in_specs=[pl.BlockSpec(memory_space=pltpu.HBM)] * 2,
        scratch_shapes=[pltpu.VMEM((2, 2, deep, wide), F32), pltpu.SemaphoreType.DMA((4,))],
        compiler_params=SMALL,
        name="faces",
    )(in_hbm(heat), in_hbm(blend))


def split3(values):
    high = values.astype(jnp.bfloat16).astype(F32)
    rest = values - high
    middle = rest.astype(jnp.bfloat16).astype(F32)
    return [high, middle, rest - middle]


def brick_kernel(
    spacing, order, far_weights, far_light, heat, blend, filled, flat, x_own, y_b, z_b, z_a,
    image, x_step, veil, weights, light, arrived,
):
    deep, tall, wide = heat.shape
    copies = [
        pltpu.make_async_copy(far_weights, weights, arrived.at[0]),
        pltpu.make_async_copy(far_light, light, arrived.at[1]),
    ]
    for copy in copies:
        copy.start()
    at = []
    for axis in ("gx", "gy", "gz"):
        at += [lax.axis_index(axis) == 0, lax.axis_index(axis) == lax.axis_size(axis) - 1]
    odd_y, odd_z = odd_place("gy"), odd_place("gz")
    column, columns = lax.axis_index("gx"), lax.axis_size("gx")
    core = lax.axis_index("gy") % 2
    left = seat(lax.rem(column + columns - 1, columns), core, columns)
    right = seat(lax.rem(column + 1, columns), core, columns)
    y_a = flat.at[seat(column, 1 - core, columns)]
    parts = deep * tall // wide
    sides = []
    for edge, place in ((at[0], left), (at[1], right)):
        for f in range(2):
            face = jnp.where(edge, x_own[f], flat[place, f, 0:deep, :])
            sides.append(jnp.concatenate([face[p : p + 1] for p in range(parts)], axis=1))
    sides = jnp.concatenate(sides + [jnp.zeros((4, deep * tall), F32)], axis=0)
    sides = jnp.concatenate(split3(sides) + [jnp.zeros_like(sides)], axis=0).astype(jnp.bfloat16)
    row = lax.broadcasted_iota(jnp.int32, (32, 2 * wide), 0)
    side = row % 8
    column = lax.broadcasted_iota(jnp.int32, (32, 2 * wide), 1)
    spread = jnp.where(
        (side < 2) & (column == side * wide), -1.0,
        jnp.where((side >= 2) & (side < 4) & (column == (side - 2) * wide + wide - 1), 1.0, 0.0),
    ).astype(jnp.bfloat16)
    across = (((0,), (0,)), ((), ()))
    x_step[...] = lax.dot_general(sides, spread, across, preferred_element_type=F32)
    slab = lax.broadcasted_iota(jnp.int32, (deep, deep * wide), 0)
    column = lax.broadcasted_iota(jnp.int32, (deep, deep * wide), 1)
    same = (column // wide == slab).astype(F32)
    veil[...] = lax.dot_general(
        filled[...].astype(F32), same, across, preferred_element_type=F32
    ) * (-spacing)
    for copy in copies:
        copy.wait()
    half = [0.5, 0.5, 0.5, 1.0]
    w = [[weights[r, k] * half[r] for k in range(7)] for r in range(4)]
    base = [w[r][6] + w[r][2] + w[r][3] for r in range(4)]
    sun = [light[i] * 0.5 for i in range(3)]
    fields = (heat, blend)
    lane8 = lax.broadcasted_iota(jnp.int32, (8, wide), 1)
    not_first = lane8 > 0
    not_last = lane8 < wide - 1
    for block in range(tall // 8):
        top = 8 * block
        rows = slice(top, top + 8)
        through = jnp.ones((8, wide), F32)
        sums = [jnp.zeros((8, wide), F32) for _ in range(4)]

        def cells(index, z):
            if z < 0:
                other = jnp.where(odd_z, z_a[index, rows, :], z_b[index, rows, :])
                return jnp.where(at[4], fields[index][0, rows, :], other)
            if z == deep:
                other = jnp.where(odd_z, z_b[index, rows, :], z_a[index, rows, :])
                return jnp.where(at[5], fields[index][deep - 1, rows, :], other)
            return fields[index][z, rows, :]

        for z in range(deep):
            slopes = []
            for index in range(2):
                field = fields[index]
                here = field[z, rows, :]
                dz = cells(index, z + 1) - cells(index, z - 1)
                if block == 0:
                    edge = jnp.where(odd_y, y_a[index, z : z + 1, :], y_b[index, z : z + 1, :])
                    edge = jnp.where(at[2], field[z, 0:1, :], edge)
                    up = jnp.concatenate([edge, field[z, 0:7, :]], axis=0)
                else:
                    up = field[z, top - 1 : top + 7, :]
                if top + 8 == tall:
                    edge = jnp.where(odd_y, y_b[index, z : z + 1, :], y_a[index, z : z + 1, :])
                    edge = jnp.where(at[3], field[z, tall - 1 : tall, :], edge)
                    down = jnp.concatenate([field[z, top + 1 : tall, :], edge], axis=0)
                else:
                    down = field[z, top + 1 : top + 9, :]
                dy = down - up
                right = jnp.where(not_last, pltpu.roll(here, wide - 1, 1), 0.0)
                left = jnp.where(not_first, pltpu.roll(here, 1, 1), 0.0)
                outer = x_step[z * tall + top : z * tall + top + 8, index * wide : (index + 1) * wide]
                dx = right - left + outer
                slopes.append((here, dz, dy, dx))
            t, tz, ty, tx = slopes[0]
            m, mz, my, mx = slopes[1]
            t_sq = tz * tz + ty * ty + tx * tx
            m_sq = mz * mz + my * my + mx * mx
            t_inverse = lax.rsqrt(t_sq * 0.25 + 1.0)
            m_inverse = lax.rsqrt(m_sq * 0.25 + 1.0)
            t_rest = t_inverse * t_inverse
            m_rest = m_inverse * m_inverse
            lit = (tx * sun[0] + ty * sun[1] + tz * sun[2]) * t_inverse
            both = t * m
            linear = [
                (base[r] + w[r][0] * t)
                + (w[r][1] * m + w[r][5] * both)
                + (w[r][4] * lit - (w[r][2] * t_rest + w[r][3] * m_rest))
                for r in range(4)
            ]
            soft = jnp.maximum(linear[3], 0.0) + jnp.log(1.0 + jnp.exp(-jnp.abs(linear[3])))
            kept = jnp.exp(soft * veil[rows, z * wide : (z + 1) * wide])
            weight = (1.0 - kept) * through
            through = through * kept
            for r in range(3):
                sums[r] = sums[r] + weight * jnp.tanh(linear[r])
            sums[3] = sums[3] + weight
        for r in range(3):
            sums[r] = 0.5 * (sums[r] + sums[3])
        for j in range(4):
            for r in range(4):
                image[order[4 * block + j], 2 * r : 2 * r + 2, :] = sums[r][2 * j : 2 * j + 2]


def over_kernel(order, parts, out):
    count, rows, wide = parts.shape
    row = lax.broadcasted_iota(jnp.int32, (8, wide), 0)
    for top in range(0, rows, 8):
        through = jnp.ones((8, wide), F32)
        total = jnp.zeros((8, wide), F32)
        for i in range(count):
            part = parts[order[i], top : top + 8, :]
            veil = jnp.where(row >= 6, part, 0.0)
            veil = veil + pltpu.roll(veil, 4, 0)
            veil = veil + pltpu.roll(veil, 2, 0)
            total = total + through * part
            through = through * (1.0 - veil)
        if out.shape[0] == 4:
            for r in range(4):
                out[r] = total[2 * r : 2 * r + 2]
        else:
            out[top : top + 8, :] = total


def over(parts, order, shape):
    def kernel(*refs):
        over_kernel(order, *refs)

    return pl.pallas_call(
        kernel, out_shape=jax.ShapeDtypeStruct(shape, F32), compiler_params=SMALL, name="over"
    )(parts)


def on_device(heat, blend, filled, weights, light):
    deep, tall, wide = heat.shape
    depth_count = lax.axis_size("gz")
    spacing = 2.0 / (deep * depth_count)
    heat, blend, flat, x_own, y_b, z_a, z_b = faces(heat, blend)
    flat = lax.all_to_all(
        flat, ("gx", "gy"), 0, 0, tiled=True,
        axis_index_groups=seats(lax.axis_size("gx"), lax.axis_size("gy")),
    )
    swap = {
        axis: [(i, ((i + 1) ^ 1) - 1) for i in range(1, lax.axis_size(axis) - 1)]
        for axis in ("gy", "gz")
    }
    y_b = lax.ppermute(y_b, "gy", swap["gy"])
    z_a = lax.ppermute(z_a, "gz", [(i, i ^ 1) for i in range(depth_count)])
    z_b = lax.ppermute(z_b, "gz", swap["gz"])
    near = 4
    near_turn = [2, 1, 0, 3]
    far = depth_count // near
    turn = [(far // 2 + i) % far for i in range(far)]
    far_order = [turn.index(i) for i in range(far)]
    near_order = [near_turn.index(k) for k in range(near)]
    near_groups = [[near * i + k for k in near_turn] for i in range(far)]
    far_groups = [[near * i + k for i in turn] for k in range(near)]
    order = [near_order[z % near] * far + far_order[z // near] for z in range(depth_count)]
    hbm = pl.BlockSpec(memory_space=pltpu.HBM)
    vmem = pl.BlockSpec(memory_space=pltpu.VMEM)

    def brick(*refs):
        brick_kernel(spacing, order, *refs)

    image = pl.pallas_call(
        brick,
        out_shape=jax.ShapeDtypeStruct((depth_count, 8, wide), F32),
        in_specs=[hbm] * 2 + [vmem] * 8,
        scratch_shapes=[
            pltpu.VMEM((deep * tall, 2 * wide), F32),
            pltpu.VMEM((tall, deep * wide), F32),
            pltpu.SMEM(weights.shape, F32),
            pltpu.SMEM(light.shape, F32),
            pltpu.SemaphoreType.DMA((2,)),
        ],
        compiler_params=SMALL,
        name="brick",
    )(in_hbm(weights), in_hbm(light), heat, blend, filled.reshape(deep, tall), flat, x_own, y_b, z_b, z_a)
    parts = lax.all_to_all(image, "gz", 0, 0, tiled=True, axis_index_groups=near_groups)
    joined = over(parts.reshape(near, far * 8, wide), near_order, (far * 8, wide))
    parts = lax.all_to_all(
        joined.reshape(far, 8, wide), "gz", 0, 0, tiled=True, axis_index_groups=far_groups
    )
    return over(parts, far_order, (4, tall // depth_count, wide))


def solution(mesh):
    placed = (P("gz", "gy", "gx"), P("gz", "gy", "gx"), P("gz", "gy", "gx"), P(), P())
    return jax.shard_map(
        on_device,
        mesh=mesh,
        in_specs=placed,
        out_specs=P(None, ("gy", "gz"), "gx"),
        check_vma=False,
    )
```

```python
import jax
import jax.numpy as jnp
from jax import lax
from jax.experimental import pallas as pl
from jax.experimental.pallas import tpu as pltpu
from jax.sharding import PartitionSpec as P

F32 = jnp.float32
SMALL = pltpu.CompilerParams(vmem_limit_bytes=8 * 2**20)


def in_hbm(array):
    return pltpu.with_memory_space_constraint(array, pltpu.HBM)


def odd_place(axis):
    return lax.axis_index(axis) % 2 == 1


def seat(column, core, columns):
    return lax.rem(column + columns - 1, columns) * 2 + 1 - core


def seats(columns, rows):
    return [
        [(i + 1) % columns * rows + 2 * chip + core for i in range(columns) for core in (1, 0)]
        for chip in range(rows // 2)
    ]


def face_kernel(
    far_heat, far_blend, heat, blend, flat, x_own, y_b, z_a, z_b, x_faces, arrived
):
    deep, tall, wide = heat.shape
    halves = [slice(0, deep // 2), slice(deep // 2, deep)]
    copies = [
        [
            pltpu.make_async_copy(far.at[half], near.at[half], arrived.at[2 * h + f])
            for f, (far, near) in enumerate(((far_heat, heat), (far_blend, blend)))
        ]
        for h, half in enumerate(halves)
    ]
    for pair in copies:
        for copy in pair:
            copy.start()
    x_faces[...] = jnp.zeros_like(x_faces)
    odd_y, odd_z = odd_place("gy"), odd_place("gz")
    lane = lax.broadcasted_iota(jnp.int32, (wide, wide), 1)
    slabs = wide // tall
    parts = deep * tall // wide
    for part in range(parts):
        if part % (parts // 2) == 0:
            for copy in copies[part // (parts // 2)]:
                copy.wait()
        t = heat[slabs * part : slabs * (part + 1)].reshape(wide, wide)
        m = blend[slabs * part : slabs * (part + 1)].reshape(wide, wide)
        ends = jnp.where(lane == 0, t, pltpu.roll(t, 2, 1))
        more = jnp.where(lane == 2, pltpu.roll(m, 2, 1), pltpu.roll(m, 4, 1))
        turned = jnp.where(lane < 2, ends, more).T
        for f in range(2):
            for side in range(2):
                at = 2 * f + side
                x_faces[side, f, part : part + 1, :] = turned[at : at + 1]
    column, columns = lax.axis_index("gx"), lax.axis_size("gx")
    core = lax.axis_index("gy") % 2
    for f, field in enumerate((heat, blend)):
        low, high = field[0], field[deep - 1]
        z_a[f] = jnp.where(odd_z, low, high)
        z_b[f] = jnp.where(odd_z, high, low)
        low = jnp.concatenate([field[z, 0:1, :] for z in range(deep)], axis=0)
        high = jnp.concatenate([field[z, tall - 1 : tall, :] for z in range(deep)], axis=0)
        y_b[f] = jnp.where(odd_y, high, low)
        beside = jnp.where(odd_y, low, high)
        left, right = x_faces[0, f], x_faces[1, f]
        x_own[f] = jnp.where(column == 0, left, right)
        for i in range(columns):
            other = (i + 1) % columns
            along = jnp.where(column < other, right, left)
            for place, its in ((2 * i, 1), (2 * i + 1, 0)):
                flat[place, f, 0:deep, :] = jnp.where(core == its, along, beside)
                flat[place, f, deep:, :] = jnp.zeros((deep, wide), F32)


def faces(heat, blend):
    deep, tall, wide = heat.shape
    members = 2 * lax.axis_size("gx")
    shapes = [heat.shape] * 2 + [(members, 2, 2 * deep, wide)] + [(2, deep, wide)] * 2
    shapes += [(2, tall, wide)] * 2
    return pl.pallas_call(
        face_kernel,
        out_shape=[jax.ShapeDtypeStruct(s, F32) for s in shapes],
        in_specs=[pl.BlockSpec(memory_space=pltpu.HBM)] * 2,
        scratch_shapes=[pltpu.VMEM((2, 2, deep, wide), F32), pltpu.SemaphoreType.DMA((4,))],
        compiler_params=SMALL,
        name="faces",
    )(in_hbm(heat), in_hbm(blend))


def split3(values):
    high = values.astype(jnp.bfloat16).astype(F32)
    rest = values - high
    middle = rest.astype(jnp.bfloat16).astype(F32)
    return [high, middle, rest - middle]


def table(weights, light):
    return [
        pltpu.SMEM(weights.shape, F32),
        pltpu.SMEM(light.shape, F32),
        pltpu.SemaphoreType.DMA((4,)),
    ]


def fetch(far_weights, far_light, weights, light, arrived):
    copies = [
        pltpu.make_async_copy(far_weights, weights, arrived.at[0]),
        pltpu.make_async_copy(far_light, light, arrived.at[1]),
    ]
    for copy in copies:
        copy.start()
    return copies


def edges(axis):
    place = lax.axis_index(axis)
    return [place == 0, place == lax.axis_size(axis) - 1]


def inner_kernel(
    spacing, order, far_weights, far_light, heat, blend, filled, flat, x_own, z_b, z_a,
    image, x_step, veil, near_weights, near_light, weights, light, arrived,
):
    deep, tall, wide = heat.shape
    copies = fetch(far_weights, far_light, weights, light, arrived)
    copies += fetch(far_weights, far_light, near_weights, near_light, arrived.at[2:])
    first, last = edges("gx")
    column, columns = lax.axis_index("gx"), lax.axis_size("gx")
    core = lax.axis_index("gy") % 2
    left = seat(lax.rem(column + columns - 1, columns), core, columns)
    right = seat(lax.rem(column + 1, columns), core, columns)
    parts = deep * tall // wide
    sides = []
    for edge, place in ((first, left), (last, right)):
        for f in range(2):
            face = jnp.where(edge, x_own[f], flat[place, f, 0:deep, :])
            sides.append(jnp.concatenate([face[p : p + 1] for p in range(parts)], axis=1))
    sides = jnp.concatenate(sides + [jnp.zeros((4, deep * tall), F32)], axis=0)
    sides = jnp.concatenate(split3(sides) + [jnp.zeros_like(sides)], axis=0).astype(jnp.bfloat16)
    row = lax.broadcasted_iota(jnp.int32, (32, 2 * wide), 0)
    side = row % 8
    column = lax.broadcasted_iota(jnp.int32, (32, 2 * wide), 1)
    spread = jnp.where(
        (side < 2) & (column == side * wide), -1.0,
        jnp.where((side >= 2) & (side < 4) & (column == (side - 2) * wide + wide - 1), 1.0, 0.0),
    ).astype(jnp.bfloat16)
    across = (((0,), (0,)), ((), ()))
    x_step[...] = lax.dot_general(sides, spread, across, preferred_element_type=F32)
    slab = lax.broadcasted_iota(jnp.int32, (deep, deep * wide), 0)
    column = lax.broadcasted_iota(jnp.int32, (deep, deep * wide), 1)
    same = (column // wide == slab).astype(F32)
    veil[...] = lax.dot_general(
        filled[...].astype(F32), same, across, preferred_element_type=F32
    ) * (-spacing)
    for copy in copies:
        copy.wait()
    blocks = range(1, tall // 8 - 1)
    rays(order, blocks, weights, light, heat, blend, None, None, z_a, z_b, x_step, veil, image)


def outer_kernel(
    order, far_weights, far_light, heat, blend, flat, y_b, z_b, z_a, part, x_step, veil,
    image, weights, light, arrived,
):
    deep, tall, wide = heat.shape
    copies = fetch(far_weights, far_light, weights, light, arrived)
    last = tall // 8 - 1
    for chunk in range(4, 4 * last):
        image[order[chunk]] = part[order[chunk]]
    core = lax.axis_index("gy") % 2
    y_a = flat.at[seat(lax.axis_index("gx"), 1 - core, lax.axis_size("gx"))]
    for copy in copies:
        copy.wait()
    blocks = (0, last)
    rays(order, blocks, weights, light, heat, blend, y_a, y_b, z_a, z_b, x_step, veil, image)


def rays(order, blocks, weights, light, heat, blend, y_a, y_b, z_a, z_b, x_step, veil, image):
    deep, tall, wide = heat.shape
    odd_y, odd_z = odd_place("gy"), odd_place("gz")
    at = edges("gx") + edges("gy") + edges("gz")
    half = [0.5, 0.5, 0.5, 1.0]
    w = [[weights[r, k] * half[r] for k in range(7)] for r in range(4)]
    base = [w[r][6] + w[r][2] + w[r][3] for r in range(4)]
    sun = [light[i] * 0.5 for i in range(3)]
    fields = (heat, blend)
    lane8 = lax.broadcasted_iota(jnp.int32, (8, wide), 1)
    not_first = lane8 > 0
    not_last = lane8 < wide - 1
    for block in blocks:
        top = 8 * block
        rows = slice(top, top + 8)
        through = jnp.ones((8, wide), F32)
        sums = [jnp.zeros((8, wide), F32) for _ in range(4)]

        def cells(index, z):
            if z < 0:
                other = jnp.where(odd_z, z_a[index, rows, :], z_b[index, rows, :])
                return jnp.where(at[4], fields[index][0, rows, :], other)
            if z == deep:
                other = jnp.where(odd_z, z_b[index, rows, :], z_a[index, rows, :])
                return jnp.where(at[5], fields[index][deep - 1, rows, :], other)
            return fields[index][z, rows, :]

        for z in range(deep):
            slopes = []
            for index in range(2):
                field = fields[index]
                here = field[z, rows, :]
                dz = cells(index, z + 1) - cells(index, z - 1)
                if block == 0:
                    edge = jnp.where(odd_y, y_a[index, z : z + 1, :], y_b[index, z : z + 1, :])
                    edge = jnp.where(at[2], field[z, 0:1, :], edge)
                    up = jnp.concatenate([edge, field[z, 0:7, :]], axis=0)
                else:
                    up = field[z, top - 1 : top + 7, :]
                if top + 8 == tall:
                    edge = jnp.where(odd_y, y_b[index, z : z + 1, :], y_a[index, z : z + 1, :])
                    edge = jnp.where(at[3], field[z, tall - 1 : tall, :], edge)
                    down = jnp.concatenate([field[z, top + 1 : tall, :], edge], axis=0)
                else:
                    down = field[z, top + 1 : top + 9, :]
                dy = down - up
                right = jnp.where(not_last, pltpu.roll(here, wide - 1, 1), 0.0)
                left = jnp.where(not_first, pltpu.roll(here, 1, 1), 0.0)
                outer = x_step[z * tall + top : z * tall + top + 8, index * wide : (index + 1) * wide]
                dx = right - left + outer
                slopes.append((here, dz, dy, dx))
            t, tz, ty, tx = slopes[0]
            m, mz, my, mx = slopes[1]
            t_sq = tz * tz + ty * ty + tx * tx
            m_sq = mz * mz + my * my + mx * mx
            t_inverse = lax.rsqrt(t_sq * 0.25 + 1.0)
            m_inverse = lax.rsqrt(m_sq * 0.25 + 1.0)
            t_rest = t_inverse * t_inverse
            m_rest = m_inverse * m_inverse
            lit = (tx * sun[0] + ty * sun[1] + tz * sun[2]) * t_inverse
            both = t * m
            linear = [
                (base[r] + w[r][0] * t)
                + (w[r][1] * m + w[r][5] * both)
                + (w[r][4] * lit - (w[r][2] * t_rest + w[r][3] * m_rest))
                for r in range(4)
            ]
            soft = jnp.maximum(linear[3], 0.0) + jnp.log(1.0 + jnp.exp(-jnp.abs(linear[3])))
            kept = jnp.exp(soft * veil[rows, z * wide : (z + 1) * wide])
            weight = (1.0 - kept) * through
            through = through * kept
            for r in range(3):
                sums[r] = sums[r] + weight * jnp.tanh(linear[r])
            sums[3] = sums[3] + weight
        for r in range(3):
            sums[r] = 0.5 * (sums[r] + sums[3])
        for j in range(4):
            for r in range(4):
                image[order[4 * block + j], 2 * r : 2 * r + 2, :] = sums[r][2 * j : 2 * j + 2]


def over_kernel(order, parts, out):
    count, rows, wide = parts.shape
    row = lax.broadcasted_iota(jnp.int32, (8, wide), 0)
    for top in range(0, rows, 8):
        through = jnp.ones((8, wide), F32)
        total = jnp.zeros((8, wide), F32)
        for i in range(count):
            part = parts[order[i], top : top + 8, :]
            veil = jnp.where(row >= 6, part, 0.0)
            veil = veil + pltpu.roll(veil, 4, 0)
            veil = veil + pltpu.roll(veil, 2, 0)
            total = total + through * part
            through = through * (1.0 - veil)
        if out.shape[0] == 4:
            for r in range(4):
                out[r] = total[2 * r : 2 * r + 2]
        else:
            out[top : top + 8, :] = total


def over(parts, order, shape):
    def kernel(*refs):
        over_kernel(order, *refs)

    return pl.pallas_call(
        kernel, out_shape=jax.ShapeDtypeStruct(shape, F32), compiler_params=SMALL, name="over"
    )(parts)


def on_device(heat, blend, filled, weights, light):
    deep, tall, wide = heat.shape
    depth_count = lax.axis_size("gz")
    spacing = 2.0 / (deep * depth_count)
    heat, blend, flat, x_own, y_b, z_a, z_b = faces(heat, blend)
    flat = lax.all_to_all(
        flat, ("gx", "gy"), 0, 0, tiled=True,
        axis_index_groups=seats(lax.axis_size("gx"), lax.axis_size("gy")),
    )
    swap = {
        axis: [(i, ((i + 1) ^ 1) - 1) for i in range(1, lax.axis_size(axis) - 1)]
        for axis in ("gy", "gz")
    }
    y_b = lax.ppermute(y_b, "gy", swap["gy"])
    z_a = lax.ppermute(z_a, "gz", [(i, i ^ 1) for i in range(depth_count)])
    z_b = lax.ppermute(z_b, "gz", swap["gz"])
    near = 4
    near_turn = [2, 1, 0, 3]
    far = depth_count // near
    turn = [(far // 2 + i) % far for i in range(far)]
    far_order = [turn.index(i) for i in range(far)]
    near_order = [near_turn.index(k) for k in range(near)]
    near_groups = [[near * i + k for k in near_turn] for i in range(far)]
    far_groups = [[near * i + k for i in turn] for k in range(near)]
    order = [near_order[z % near] * far + far_order[z // near] for z in range(depth_count)]
    hbm = pl.BlockSpec(memory_space=pltpu.HBM)
    vmem = pl.BlockSpec(memory_space=pltpu.VMEM)

    def inner(*refs):
        inner_kernel(spacing, order, *refs)

    def outer(*refs):
        outer_kernel(order, *refs)

    weights, light = in_hbm(weights), in_hbm(light)
    shape = jax.ShapeDtypeStruct((depth_count, 8, wide), F32)
    cells = deep * tall * wide
    part, x_step, veil, near_weights, near_light = pl.pallas_call(
        inner,
        out_shape=[
            shape,
            jax.ShapeDtypeStruct((deep * tall, 2 * wide), F32),
            jax.ShapeDtypeStruct((tall, deep * wide), F32),
            jax.ShapeDtypeStruct(weights.shape, F32),
            jax.ShapeDtypeStruct(light.shape, F32),
        ],
        in_specs=[hbm] * 2 + [vmem] * 7,
        scratch_shapes=table(weights, light),
        compiler_params=SMALL,
        cost_estimate=pl.CostEstimate(
            flops=120 * cells, bytes_accessed=8 * cells, transcendentals=8 * cells
        ),
        name="inner",
    )(weights, light, heat, blend, filled.reshape(deep, tall), flat, x_own, z_b, z_a)
    image = pl.pallas_call(
        outer,
        out_shape=shape,
        in_specs=[vmem] * 11,
        scratch_shapes=table(weights, light),
        compiler_params=SMALL,
        name="outer",
    )(near_weights, near_light, heat, blend, flat, y_b, z_b, z_a, part, x_step, veil)
    parts = lax.all_to_all(image, "gz", 0, 0, tiled=True, axis_index_groups=near_groups)
    joined = over(parts.reshape(near, far * 8, wide), near_order, (far * 8, wide))
    parts = lax.all_to_all(
        joined.reshape(far, 8, wide), "gz", 0, 0, tiled=True, axis_index_groups=far_groups
    )
    return over(parts, far_order, (4, tall // depth_count, wide))


def solution(mesh):
    placed = (P("gz", "gy", "gx"), P("gz", "gy", "gx"), P("gz", "gy", "gx"), P(), P())
    return jax.shard_map(
        on_device,
        mesh=mesh,
        in_specs=placed,
        out_specs=P(None, ("gy", "gz"), "gx"),
        check_vma=False,
    )
```

```python
import jax
import jax.numpy as jnp
from jax import lax
from jax.experimental import pallas as pl
from jax.experimental.pallas import tpu as pltpu
from jax.sharding import PartitionSpec as P

F32 = jnp.float32
SMALL = pltpu.CompilerParams(vmem_limit_bytes=8 * 2**20)


def in_hbm(array):
    return pltpu.with_memory_space_constraint(array, pltpu.HBM)


def odd_place(axis):
    return lax.axis_index(axis) % 2 == 1


def seat(column, core, columns):
    return lax.rem(column + columns - 1, columns) * 2 + 1 - core


def seats(columns, rows):
    return [
        [(i + 1) % columns * rows + 2 * chip + core for i in range(columns) for core in (1, 0)]
        for chip in range(rows // 2)
    ]


def face_kernel(
    far_heat, far_blend, heat, blend, flat, x_own, y_b, z_a, z_b, x_faces, arrived
):
    deep, tall, wide = heat.shape
    halves = [slice(0, deep // 2), slice(deep // 2, deep)]
    copies = [
        [
            pltpu.make_async_copy(far.at[half], near.at[half], arrived.at[2 * h + f])
            for f, (far, near) in enumerate(((far_heat, heat), (far_blend, blend)))
        ]
        for h, half in enumerate(halves)
    ]
    for pair in copies:
        for copy in pair:
            copy.start()
    x_faces[...] = jnp.zeros_like(x_faces)
    odd_y, odd_z = odd_place("gy"), odd_place("gz")
    lane = lax.broadcasted_iota(jnp.int32, (wide, wide), 1)
    slabs = wide // tall
    parts = deep * tall // wide
    for part in range(parts):
        if part % (parts // 2) == 0:
            for copy in copies[part // (parts // 2)]:
                copy.wait()
        t = heat[slabs * part : slabs * (part + 1)].reshape(wide, wide)
        m = blend[slabs * part : slabs * (part + 1)].reshape(wide, wide)
        ends = jnp.where(lane == 0, t, pltpu.roll(t, 2, 1))
        more = jnp.where(lane == 2, pltpu.roll(m, 2, 1), pltpu.roll(m, 4, 1))
        turned = jnp.where(lane < 2, ends, more).T
        for f in range(2):
            for side in range(2):
                at = 2 * f + side
                x_faces[side, f, part : part + 1, :] = turned[at : at + 1]
    flat[:, 2] = jnp.zeros((flat.shape[0], deep, wide), F32)
    column, columns = lax.axis_index("gx"), lax.axis_size("gx")
    core = lax.axis_index("gy") % 2
    for f, field in enumerate((heat, blend)):
        low, high = field[0], field[deep - 1]
        z_a[f] = jnp.where(odd_z, low, high)
        z_b[f] = jnp.where(odd_z, high, low)
        low = jnp.concatenate([field[z, 0:1, :] for z in range(deep)], axis=0)
        high = jnp.concatenate([field[z, tall - 1 : tall, :] for z in range(deep)], axis=0)
        y_b[f] = jnp.where(odd_y, high, low)
        beside = jnp.where(odd_y, low, high)
        left, right = x_faces[0, f], x_faces[1, f]
        x_own[0, f] = left
        x_own[1, f] = right
        for i in range(columns):
            other = (i + 1) % columns
            along = jnp.where(column < other, right, left)
            for place, its in ((2 * i, 1), (2 * i + 1, 0)):
                flat[place, f] = jnp.where(core == its, along, beside)


def faces(heat, blend):
    deep, tall, wide = heat.shape
    members = 2 * lax.axis_size("gx")
    shapes = [heat.shape] * 2 + [(members, 3, deep, wide), (2, 2, deep, wide), (2, deep, wide)]
    shapes += [(2, tall, wide)] * 2
    return pl.pallas_call(
        face_kernel,
        out_shape=[jax.ShapeDtypeStruct(s, F32) for s in shapes],
        in_specs=[pl.BlockSpec(memory_space=pltpu.HBM)] * 2,
        scratch_shapes=[pltpu.VMEM((2, 2, deep, wide), F32), pltpu.SemaphoreType.DMA((4,))],
        compiler_params=SMALL,
        name="faces",
    )(in_hbm(heat), in_hbm(blend))


def split3(values):
    high = values.astype(jnp.bfloat16).astype(F32)
    rest = values - high
    middle = rest.astype(jnp.bfloat16).astype(F32)
    return [high, middle, rest - middle]


def table(weights, light):
    return [
        pltpu.SMEM(weights.shape, F32),
        pltpu.SMEM(light.shape, F32),
        pltpu.SemaphoreType.DMA((4,)),
    ]


def fetch(far_weights, far_light, weights, light, arrived):
    copies = [
        pltpu.make_async_copy(far_weights, weights, arrived.at[0]),
        pltpu.make_async_copy(far_light, light, arrived.at[1]),
    ]
    for copy in copies:
        copy.start()
    return copies


def edges(axis):
    place = lax.axis_index(axis)
    return [place == 0, place == lax.axis_size(axis) - 1]


def inner_kernel(
    spacing, order, far_weights, far_light, heat, blend, filled, flat, x_own, z_b, z_a,
    image, x_step, veil, near_weights, near_light, weights, light, arrived,
):
    deep, tall, wide = heat.shape
    copies = fetch(far_weights, far_light, weights, light, arrived)
    copies += fetch(far_weights, far_light, near_weights, near_light, arrived.at[2:])
    first, last = edges("gx")
    column, columns = lax.axis_index("gx"), lax.axis_size("gx")
    core = lax.axis_index("gy") % 2
    left = seat(lax.rem(column + columns - 1, columns), core, columns)
    right = seat(lax.rem(column + 1, columns), core, columns)
    parts = deep * tall // wide
    sides = []
    for side, edge, place in ((0, first, left), (1, last, right)):
        for f in range(2):
            face = jnp.where(edge, x_own[side, f], flat[place, f]) - x_own[1 - side, f]
            sides.append(jnp.concatenate([face[p : p + 1] for p in range(parts)], axis=1))
    sides = jnp.concatenate(sides + [jnp.zeros((4, deep * tall), F32)], axis=0)
    sides = jnp.concatenate(split3(sides) + [jnp.zeros_like(sides)], axis=0).astype(jnp.bfloat16)
    row = lax.broadcasted_iota(jnp.int32, (32, 2 * wide), 0)
    side = row % 8
    column = lax.broadcasted_iota(jnp.int32, (32, 2 * wide), 1)
    spread = jnp.where(
        (side < 2) & (column == side * wide), -1.0,
        jnp.where((side >= 2) & (side < 4) & (column == (side - 2) * wide + wide - 1), 1.0, 0.0),
    ).astype(jnp.bfloat16)
    across = (((0,), (0,)), ((), ()))
    x_step[...] = lax.dot_general(sides, spread, across, preferred_element_type=F32)
    slab = lax.broadcasted_iota(jnp.int32, (deep, deep * wide), 0)
    column = lax.broadcasted_iota(jnp.int32, (deep, deep * wide), 1)
    same = (column // wide == slab).astype(F32)
    veil[...] = lax.dot_general(
        filled[...].astype(F32), same, across, preferred_element_type=F32
    ) * (-spacing)
    for copy in copies:
        copy.wait()
    blocks = range(1, tall // 8 - 1)
    rays(order, blocks, weights, light, heat, blend, None, None, z_a, z_b, x_step, veil, image)


def outer_kernel(
    order, far_weights, far_light, heat, blend, flat, y_b, z_b, z_a, part, x_step, veil,
    image, weights, light, arrived,
):
    deep, tall, wide = heat.shape
    copies = fetch(far_weights, far_light, weights, light, arrived)
    last = tall // 8 - 1
    for chunk in range(4, 4 * last):
        image[order[chunk]] = part[order[chunk]]
    core = lax.axis_index("gy") % 2
    y_a = flat.at[seat(lax.axis_index("gx"), 1 - core, lax.axis_size("gx"))]
    for copy in copies:
        copy.wait()
    blocks = (0, last)
    rays(order, blocks, weights, light, heat, blend, y_a, y_b, z_a, z_b, x_step, veil, image)


def rays(order, blocks, weights, light, heat, blend, y_a, y_b, z_a, z_b, x_step, veil, image):
    deep, tall, wide = heat.shape
    odd_y, odd_z = odd_place("gy"), odd_place("gz")
    at = edges("gx") + edges("gy") + edges("gz")
    half = [0.5, 0.5, 0.5, 1.0]
    w = [[weights[r, k] * half[r] for k in range(7)] for r in range(4)]
    base = [w[r][6] + w[r][2] + w[r][3] for r in range(4)]
    sun = [light[i] * 0.5 for i in range(3)]
    fields = (heat, blend)
    for block in blocks:
        top = 8 * block
        rows = slice(top, top + 8)
        through = jnp.ones((8, wide), F32)
        sums = [jnp.zeros((8, wide), F32) for _ in range(4)]

        def cells(index, z):
            if z < 0:
                other = jnp.where(odd_z, z_a[index, rows, :], z_b[index, rows, :])
                return jnp.where(at[4], fields[index][0, rows, :], other)
            if z == deep:
                other = jnp.where(odd_z, z_b[index, rows, :], z_a[index, rows, :])
                return jnp.where(at[5], fields[index][deep - 1, rows, :], other)
            return fields[index][z, rows, :]

        for z in range(deep):
            slopes = []
            for index in range(2):
                field = fields[index]
                here = field[z, rows, :]
                dz = cells(index, z + 1) - cells(index, z - 1)
                if block == 0:
                    edge = jnp.where(odd_y, y_a[index, z : z + 1, :], y_b[index, z : z + 1, :])
                    edge = jnp.where(at[2], field[z, 0:1, :], edge)
                    up = jnp.concatenate([edge, field[z, 0:7, :]], axis=0)
                else:
                    up = field[z, top - 1 : top + 7, :]
                if top + 8 == tall:
                    edge = jnp.where(odd_y, y_b[index, z : z + 1, :], y_a[index, z : z + 1, :])
                    edge = jnp.where(at[3], field[z, tall - 1 : tall, :], edge)
                    down = jnp.concatenate([field[z, top + 1 : tall, :], edge], axis=0)
                else:
                    down = field[z, top + 1 : top + 9, :]
                dy = down - up
                right = pltpu.roll(here, wide - 1, 1)
                left = pltpu.roll(here, 1, 1)
                outer = x_step[z * tall + top : z * tall + top + 8, index * wide : (index + 1) * wide]
                dx = right - left + outer
                slopes.append((here, dz, dy, dx))
            t, tz, ty, tx = slopes[0]
            m, mz, my, mx = slopes[1]
            t_sq = tz * tz + ty * ty + tx * tx
            m_sq = mz * mz + my * my + mx * mx
            t_inverse = lax.rsqrt(t_sq * 0.25 + 1.0)
            m_inverse = lax.rsqrt(m_sq * 0.25 + 1.0)
            t_rest = t_inverse * t_inverse
            m_rest = m_inverse * m_inverse
            lit = (tx * sun[0] + ty * sun[1] + tz * sun[2]) * t_inverse
            both = t * m
            linear = [
                (base[r] + w[r][0] * t)
                + (w[r][1] * m + w[r][5] * both)
                + (w[r][4] * lit - (w[r][2] * t_rest + w[r][3] * m_rest))
                for r in range(4)
            ]
            soft = jnp.maximum(linear[3], 0.0) + jnp.log(1.0 + jnp.exp(-jnp.abs(linear[3])))
            kept = jnp.exp(soft * veil[rows, z * wide : (z + 1) * wide])
            weight = (1.0 - kept) * through
            through = through * kept
            for r in range(3):
                sums[r] = sums[r] + weight * jnp.tanh(linear[r])
            sums[3] = sums[3] + weight
        for r in range(3):
            sums[r] = 0.5 * (sums[r] + sums[3])
        for j in range(4):
            for r in range(4):
                image[order[4 * block + j], 2 * r : 2 * r + 2, :] = sums[r][2 * j : 2 * j + 2]


def over_kernel(order, parts, out):
    count, rows, wide = parts.shape
    row = lax.broadcasted_iota(jnp.int32, (8, wide), 0)
    for top in range(0, rows, 8):
        through = jnp.ones((8, wide), F32)
        total = jnp.zeros((8, wide), F32)
        for i in range(count):
            part = parts[order[i], top : top + 8, :]
            veil = jnp.where(row >= 6, part, 0.0)
            veil = veil + pltpu.roll(veil, 4, 0)
            veil = veil + pltpu.roll(veil, 2, 0)
            total = total + through * part
            through = through * (1.0 - veil)
        if out.shape[0] == 4:
            for r in range(4):
                out[r] = total[2 * r : 2 * r + 2]
        else:
            out[top : top + 8, :] = total


def over(parts, order, shape):
    def kernel(*refs):
        over_kernel(order, *refs)

    return pl.pallas_call(
        kernel, out_shape=jax.ShapeDtypeStruct(shape, F32), compiler_params=SMALL, name="over"
    )(parts)


def on_device(heat, blend, filled, weights, light):
    deep, tall, wide = heat.shape
    depth_count = lax.axis_size("gz")
    spacing = 2.0 / (deep * depth_count)
    heat, blend, flat, x_own, y_b, z_a, z_b = faces(heat, blend)
    flat = lax.all_to_all(
        flat, ("gx", "gy"), 0, 0, tiled=True,
        axis_index_groups=seats(lax.axis_size("gx"), lax.axis_size("gy")),
    )
    swap = {
        axis: [(i, ((i + 1) ^ 1) - 1) for i in range(1, lax.axis_size(axis) - 1)]
        for axis in ("gy", "gz")
    }
    y_b = lax.ppermute(y_b, "gy", swap["gy"])
    z_a = lax.ppermute(z_a, "gz", [(i, i ^ 1) for i in range(depth_count)])
    z_b = lax.ppermute(z_b, "gz", swap["gz"])
    near = 4
    near_turn = [2, 1, 0, 3]
    far = depth_count // near
    turn = [(far // 2 + i) % far for i in range(far)]
    far_order = [turn.index(i) for i in range(far)]
    near_order = [near_turn.index(k) for k in range(near)]
    near_groups = [[near * i + k for k in near_turn] for i in range(far)]
    far_groups = [[near * i + k for i in turn] for k in range(near)]
    order = [near_order[z % near] * far + far_order[z // near] for z in range(depth_count)]
    hbm = pl.BlockSpec(memory_space=pltpu.HBM)
    vmem = pl.BlockSpec(memory_space=pltpu.VMEM)

    def inner(*refs):
        inner_kernel(spacing, order, *refs)

    def outer(*refs):
        outer_kernel(order, *refs)

    weights, light = in_hbm(weights), in_hbm(light)
    shape = jax.ShapeDtypeStruct((depth_count, 8, wide), F32)
    cells = deep * tall * wide
    part, x_step, veil, near_weights, near_light = pl.pallas_call(
        inner,
        out_shape=[
            shape,
            jax.ShapeDtypeStruct((deep * tall, 2 * wide), F32),
            jax.ShapeDtypeStruct((tall, deep * wide), F32),
            jax.ShapeDtypeStruct(weights.shape, F32),
            jax.ShapeDtypeStruct(light.shape, F32),
        ],
        in_specs=[hbm] * 2 + [vmem] * 7,
        scratch_shapes=table(weights, light),
        compiler_params=SMALL,
        cost_estimate=pl.CostEstimate(
            flops=120 * cells, bytes_accessed=8 * cells, transcendentals=8 * cells
        ),
        name="inner",
    )(weights, light, heat, blend, filled.reshape(deep, tall), flat, x_own, z_b, z_a)
    image = pl.pallas_call(
        outer,
        out_shape=shape,
        in_specs=[vmem] * 11,
        scratch_shapes=table(weights, light),
        compiler_params=SMALL,
        name="outer",
    )(near_weights, near_light, heat, blend, flat, y_b, z_b, z_a, part, x_step, veil)
    parts = lax.all_to_all(image, "gz", 0, 0, tiled=True, axis_index_groups=near_groups)
    joined = over(parts.reshape(near, far * 8, wide), near_order, (far * 8, wide))
    parts = lax.all_to_all(
        joined.reshape(far, 8, wide), "gz", 0, 0, tiled=True, axis_index_groups=far_groups
    )
    return over(parts, far_order, (4, tall // depth_count, wide))


def solution(mesh):
    placed = (P("gz", "gy", "gx"), P("gz", "gy", "gx"), P("gz", "gy", "gx"), P(), P())
    return jax.shard_map(
        on_device,
        mesh=mesh,
        in_specs=placed,
        out_specs=P(None, ("gy", "gz"), "gx"),
        check_vma=False,
    )
```
